256 devices in a mesh: wide: 64 (over z, x_lo, y), narrow: 4 (over x_hi, core).
Axes of the slice: x: 4 (x_hi: 2, x_lo: 2; x = x_hi * 2 + x_lo), y: 4, z: 8, core: 2. Of those that a mesh axis runs over, the one named last changes fastest.
Arguments:
- parent_front: bfloat16 [196608, 5120], P('wide', 'narrow'), may hold values from -0.078125 to 0.078125
- child_updates: bfloat16 [131072, 2048], P('wide', 'narrow'), may hold values from -0.078125 to 0.078125
- child_map: int32 [131072], P('wide'), may hold values from 0 to 196607, as said below
- tile_mask: int32 [768, 40], P('wide', 'narrow'), may hold values 0 or 1
- probes: bfloat16 [5120, 512], P('narrow'), may hold values from -6 to 6
Outputs:
- probe_image: bfloat16 [196608, 512], P('wide', 'narrow')
The draws below stay inside these ranges and needn't reach their ends.
Inputs may be any that keep to these rules, and one draw needn't show every extreme that they name: `child_map`: the rows of one child go to distinct parent rows. Of the 2048 rows of one child held by one wide device, exactly 32 have parent rows on each wide device w, that is rows w * 3072 to (w + 1) * 3072 - 1.
All inputs are finite; a program needn't handle non-finite values. No bound on the sum of `tile_mask` on one device may be relied on, other than what follows from the above.
Results may differ from the reference program's by a relative error of at most 0.012.
Values may be sent and summed in bfloat16 or wider, within the bound.
No kernel may reach another device: no remote copies, remote signals or barrier semaphores. Data moves between devices by JAX's collectives and lax.ppermute only.
A program may use at most 128 MiB of HBM per device.

```python
import jax
import jax.numpy as jnp
from jax import lax

ROW_PAIR = 32
TOUCHED_DEV = 512
OWN_DEV = 768
PROBES = 512
TILE = 128
ROW_TILES = 12
CHILD_ROWS_DEV = 2048
FRONT_ROWS_DEV = 3072
ROW_TILE = 256
CHILD_ORDER = 65536
FRONT_ORDER = 196608
FRONT_COLS = 5120
CHILD_COLS = 2048
N_WIDE = 64
N_NARROW = 4


def draw_child_map(key, part):
    key = jax.random.fold_in(key, 11)
    wide_count = CHILD_ROWS_DEV // ROW_PAIR
    half_count = wide_count // 2
    key_list = jax.random.split(key, 2 * wide_count)
    chosen = jax.vmap(lambda single: jax.random.permutation(single, FRONT_ROWS_DEV)[:half_count * ROW_PAIR])(key_list)
    chosen = chosen.astype(jnp.int32).reshape(2, wide_count, half_count, ROW_PAIR)
    offsets = (jnp.arange(wide_count, dtype=jnp.int32) * FRONT_ROWS_DEV).reshape(1, wide_count, 1, 1)
    placed = (chosen + offsets).transpose(0, 2, 1, 3).reshape(2, half_count, wide_count * ROW_PAIR)
    shuffle_keys = jax.random.split(jax.random.fold_in(key, 1), 2 * half_count)
    shuffle = jax.vmap(lambda single: jax.random.permutation(single, wide_count * ROW_PAIR))(shuffle_keys)
    shuffle = shuffle.astype(jnp.int32).reshape(2, half_count, wide_count * ROW_PAIR)
    placed = jnp.take_along_axis(placed, shuffle, axis=2)
    return placed.reshape(-1).astype(jnp.int32)


def place_ends(entries, own_key, low, high):
    index_at = [jax.random.randint(jax.random.fold_in(own_key, axis), (), 0, length) for axis, length in enumerate(entries.shape)]
    widest = entries.shape.index(max(entries.shape))
    beside = index_at[:widest] + [(index_at[widest] + 1) % entries.shape[widest]] + index_at[widest + 1:]
    return entries.at[tuple(index_at)].set(low).at[tuple(beside)].set(high)


def level_of(key, extent, cuts, low, top_value):
    def one(dim, parts):
        steps = jax.random.uniform(jax.random.fold_in(jax.random.fold_in(key, 6), dim), (parts,), jnp.float32, low / len(cuts), top_value / len(cuts))
        return jnp.repeat(jnp.exp(steps), extent[dim] // parts).reshape((-1,) + (1,) * (len(extent) - dim - 1))

    loudness = one(*cuts[0])
    for cut in cuts[1:]:
        loudness = loudness * one(*cut)
    return loudness


def scatter_about(stream_key, dims, scale, reach, shards=(), held_as=jnp.bfloat16):
    level = level_of(stream_key, dims, shards, -0.22, 0.18) if shards else 1.0
    values = jax.random.normal(stream_key, dims, jnp.float32) * scale * level
    return jnp.minimum(jnp.maximum(values, -reach), reach).astype(held_as)


def setup_inputs(seed: int = 0) -> dict:
    arg_keys = jax.random.split(jax.random.key(seed), 6)
    parent_front = scatter_about(arg_keys[0], (FRONT_ORDER, FRONT_COLS), FRONT_COLS ** -0.5, 0.078125, ((0, 64), (1, 4)))
    child_updates = scatter_about(arg_keys[1], (2 * CHILD_ORDER, CHILD_COLS), FRONT_COLS ** -0.5, 0.078125, ((0, 64), (1, 4)))
    child_map = draw_child_map(jax.random.fold_in(arg_keys[5], 71), 0)
    tile_mask = place_ends((jax.random.randint(arg_keys[3], (FRONT_ORDER // ROW_TILE, FRONT_COLS // TILE), 0, 4) < 3).astype(jnp.int32), jax.random.fold_in(arg_keys[3], 1), 0, 1)
    probes = scatter_about(arg_keys[4], (FRONT_COLS, PROBES), 1.0, 6.0, ((0, 4),))
    return dict(parent_front=parent_front, child_updates=child_updates, child_map=child_map, tile_mask=tile_mask, probes=probes)


def masked_block(panel_block, mask_part):
    row_count, col_count = panel_block.shape
    tile_view = panel_block.reshape(mask_part.shape[0], row_count // mask_part.shape[0], mask_part.shape[1], col_count // mask_part.shape[1])
    return (tile_view * mask_part[:, None, :, None].astype(panel_block.dtype)).reshape(row_count, col_count)


def reference(parent_front, child_updates, child_map, tile_mask, probes):
    col_dev = TOUCHED_DEV + OWN_DEV
    child_three = child_updates.reshape(2 * CHILD_ORDER, N_NARROW, TOUCHED_DEV).astype(jnp.float32)
    added_sum = jnp.zeros((FRONT_ORDER, N_NARROW, TOUCHED_DEV), jnp.float32).at[child_map].add(child_three)
    parent_four = parent_front.reshape(N_WIDE, FRONT_ROWS_DEV, N_NARROW, col_dev)
    added_four = added_sum.reshape(N_WIDE, FRONT_ROWS_DEV, N_NARROW, TOUCHED_DEV)
    mask_four = tile_mask.reshape(N_WIDE, ROW_TILES, N_NARROW, col_dev // TILE)
    probe_three = probes.reshape(N_NARROW, col_dev, PROBES)

    def one_device(pieces):
        front_block, added_rows, mask_part = pieces
        summed = jnp.zeros((FRONT_ROWS_DEV, PROBES), jnp.float32)
        for group_index in range(N_NARROW):
            touched = (front_block[:, group_index, :TOUCHED_DEV].astype(jnp.float32) + added_rows[:, group_index]).astype(jnp.bfloat16)
            whole_panel = jnp.concatenate([touched, front_block[:, group_index, TOUCHED_DEV:]], axis=1)
            masked = masked_block(whole_panel, mask_part[:, group_index])
            partial_value = jnp.dot(masked, probe_three[group_index], preferred_element_type=jnp.float32).astype(jnp.bfloat16)
            summed = summed + lax.optimization_barrier(partial_value).astype(jnp.float32)
        return summed.astype(jnp.bfloat16)

    result = lax.map(one_device, (parent_four, added_four, mask_four))
    return result.reshape(FRONT_ORDER, PROBES)
```

```python
import jax
import jax.numpy as jnp
from jax import lax
from jax.experimental import pallas as pl
from jax.experimental.pallas import tpu as pltpu
from jax.sharding import Mesh, PartitionSpec as P

BF = jnp.bfloat16
F32 = jnp.float32
I32 = jnp.int32
ROWS = 3072
KIDS = 2048
WIDE = 64
PAIR = 32
LANES = 128
MIB = 1 << 20
WIDE_AXES = ("z", "l", "y")


def iota(shape, dim):
    return lax.broadcasted_iota(I32, shape, dim)


def params(mib):
    return pltpu.CompilerParams(vmem_limit_bytes=mib * MIB)


def split_map(child_map):
    target = (lax.shift_right_logical(child_map, 10) * 171) >> 9
    return target, child_map - target * ROWS


def rank_kernel(map_ref, mask_ref, pos_ref, out_ref, hot_ref, val_ref):
    target, place = split_map(map_ref[...])
    blocks = KIDS // LANES
    upper = (iota((LANES, 2 * LANES), 0) < iota((LANES, 2 * LANES), 1)).astype(F32).astype(BF)
    carry = jnp.zeros((WIDE, LANES), F32)
    lane_rank = (iota((LANES, LANES), 0) & (PAIR - 1)).astype(F32)
    for b in range(blocks):
        at = pl.ds(b * LANES, LANES)
        hot = (iota((WIDE, LANES), 0) == target[b : b + 1, :]).astype(F32)
        hot_ref[:, at] = hot.astype(BF)
        sums = jnp.dot(hot.astype(BF), upper, preferred_element_type=F32)
        rank = jnp.sum(hot * (sums[:, :LANES] + carry), axis=0, keepdims=True)
        carry = carry + sums[:, LANES:]
        pos_ref[b : b + 1, :] = target[b : b + 1, :] * PAIR + rank.astype(I32)
        chosen = lane_rank == rank
        high = (place[b : b + 1, :] >> 6).astype(F32)
        low = (place[b : b + 1, :] & 63).astype(F32)
        val_ref[:LANES, at] = jnp.where(chosen, high, 0.0).astype(BF)
        val_ref[LANES:, at] = jnp.where(chosen, low, 0.0).astype(BF)
    both = lax.dot_general(
        hot_ref[...], val_ref[...], (((1,), (1,)), ((), ())), preferred_element_type=F32
    )
    places = (both[:, :LANES] * 64.0 + both[:, LANES:]).astype(I32)
    lane = iota((12, LANES), 1) & 63
    row = iota((12, LANES), 0)
    flat = jnp.zeros((1, LANES), I32)
    for t in range(4):
        flat += jnp.sum(
            jnp.where(lane == row * 4 + t, mask_ref[:, t : t + 1], 0), axis=0, keepdims=True
        )
    for core in range(2):
        out_ref[:, core, 0, :] = places
        out_ref[:, core, 1, :] = jnp.broadcast_to(flat, (WIDE, LANES))


def rank_call(child_map, tile_mask):
    return pl.pallas_call(
        rank_kernel,
        out_shape=(
            jax.ShapeDtypeStruct((KIDS // LANES, LANES), I32),
            jax.ShapeDtypeStruct((WIDE, 2, 2, LANES), I32),
        ),
        scratch_shapes=[pltpu.VMEM((WIDE, KIDS), BF), pltpu.VMEM((2 * LANES, KIDS), BF)],
        compiler_params=params(58),
        cost_estimate=pl.CostEstimate(flops=1000, bytes_accessed=1000, transcendentals=0),
        name="rank",
    )(child_map, tile_mask)


def load_probes(src, dst, sem, starts, first=0, first_sem=0):
    rows = pl.ds(first, src.shape[0])
    return [
        pltpu.make_async_copy(
            src.at[:, pl.ds(pl.multiple_of(start * LANES, LANES), LANES)],
            dst.at[rows, pl.ds(k * LANES, LANES)],
            sem.at[first_sem + k],
        )
        for k, start in enumerate(starts)
    ]


PARENT_TALL = 768


def parent_kernel(
    mask_ref, x_ref, probe_ref, far_keep_ref, own_keep_ref, send_ref,
    held_ref, buf_ref, out_ref, probe_sem, sems, out_sems,
):
    h, c = lax.axis_index("h"), lax.axis_index("c")
    tall = PARENT_TALL
    chunks = ROWS // tall
    probe_copies = load_probes(
        probe_ref,
        held_ref,
        probe_sem,
        [2 * (1 - h) + c, 2 * h + c, 2 * (1 - h) + 1 - c, 2 * h + 1 - c],
    )
    reads = [
        pltpu.make_async_copy(
            x_ref.at[pl.ds(k * 256, 256)], buf_ref.at[pl.ds(k * 256, 256)], sems.at[k]
        )
        for k in range(ROWS // 256)
    ]
    step = tall // 256
    for copy in probe_copies + reads[: 2 * step]:
        copy.start()
    for copy in probe_copies:
        copy.wait()
    writes = []
    for k in range(chunks):
        for copy in reads[k * step : (k + 1) * step]:
            copy.wait()
        for copy in reads[(k + 2) * step : (k + 3) * step]:
            copy.start()
        masked = jnp.concatenate(
            [
                jnp.concatenate(
                    [
                        jnp.where(
                            mask_ref[r, t] != 0,
                            buf_ref[r * 256 : (r + 1) * 256, t * LANES : (t + 1) * LANES],
                            jnp.zeros((), BF),
                        )
                        for t in range(10)
                    ],
                    axis=1,
                )
                for r in range(k * step, (k + 1) * step)
            ],
            axis=0,
        )
        out_ref[k * tall : (k + 1) * tall, :] = jnp.dot(
            masked, held_ref[...], preferred_element_type=F32
        ).astype(BF)
        at = pl.ds(k * tall, tall)
        for n, (dst, first, wide) in enumerate(
            ((far_keep_ref, 0, LANES), (own_keep_ref, LANES, LANES), (send_ref, 256, 256))
        ):
            copy = pltpu.make_async_copy(
                out_ref.at[at, pl.ds(first, wide)], dst.at[at], out_sems.at[k, n]
            )
            copy.start()
            writes.append(copy)
    for copy in writes:
        copy.wait()


VM = pl.BlockSpec(memory_space=pltpu.VMEM)
SM = pl.BlockSpec(memory_space=pltpu.SMEM)
ANY = pl.BlockSpec(memory_space=pl.ANY)
LONG = pl.CostEstimate(flops=200 * 10**9, bytes_accessed=64 * MIB, transcendentals=0)
SHORT = pl.CostEstimate(flops=1000, bytes_accessed=1000, transcendentals=0)


def parent_call(tile_mask, front, probes):
    return pl.pallas_call(
        parent_kernel,
        in_specs=[SM, ANY, ANY],
        out_specs=[ANY] * 3,
        out_shape=[
            jax.ShapeDtypeStruct((ROWS, LANES), BF),
            jax.ShapeDtypeStruct((ROWS, LANES), BF),
            jax.ShapeDtypeStruct((ROWS, 256), BF),
        ],
        scratch_shapes=[
            pltpu.VMEM((1280, 512), BF),
            pltpu.VMEM((ROWS, 1280), BF),
            pltpu.VMEM((ROWS, 512), BF),
            pltpu.SemaphoreType.DMA((4,)),
            pltpu.SemaphoreType.DMA((ROWS // 256,)),
            pltpu.SemaphoreType.DMA((ROWS // PARENT_TALL, 3)),
        ],
        compiler_params=params(58),
        cost_estimate=LONG,
        name="parent_product",
    )(tile_mask, front, probes)


def child_kernel(
    map_ref, pos_ref, given_ref, x_ref, other_ref, probe_ref, probe2_ref,
    out_ref, held_ref, buf_ref, hot_ref, low_ref, product_ref, perm_ref, stage_ref,
    probe_sem, sems, out_sems,
):
    c = lax.axis_index("c")
    tall = 1024
    copies = load_probes(probe_ref.at[pl.ds(0, 512)], held_ref, probe_sem, [c, 2 + c])
    copies += load_probes(
        probe2_ref.at[pl.ds(0, 512)], held_ref, probe_sem, [c, 2 + c], 512, 2
    )
    reads = []
    for k in range(4):
        at = pl.ds(k * 512, 512)
        for n, src in enumerate((x_ref, other_ref)):
            reads.append(
                pltpu.make_async_copy(
                    src.at[at], buf_ref.at[at, pl.ds(n * 512, 512)], sems.at[k, n]
                )
            )
    for copy in copies + reads:
        copy.start()

    target, place = split_map(map_ref[...])
    tile = place >> 8
    pos = pos_ref[...]
    low = pos & 255
    for b in range(KIDS // LANES):
        rows = slice(b * LANES, (b + 1) * LANES)
        hot = (iota((LANES, LANES), 0) == target[b : b + 1, :]).astype(F32)
        hot_ref[rows, :LANES] = hot.T.astype(BF)
        on = (((iota((LANES, LANES), 0) & 63) >> 2) == tile[b : b + 1, :]).astype(F32)
        hot_ref[rows, LANES:] = on.T.astype(BF)
        low_ref[:, rows] = (iota((256, LANES), 0) == low[b : b + 1, :]).astype(F32).astype(BF)

    own = given_ref[:, pl.ds(c, 1), 1, :].reshape(WIDE, LANES)
    other = given_ref[:, pl.ds(1 - c, 1), 1, :].reshape(WIDE, LANES)
    mask = jnp.where(iota((WIDE, LANES), 1) < 64, own, other).astype(F32).astype(BF)
    mask = jnp.concatenate([mask, jnp.zeros((WIDE, LANES), BF)], axis=0)
    lane, col = iota((LANES, 1024), 0), iota((LANES, 1024), 1)
    expand = ((lane >> 6) * 4 + (lane & 3) == (col >> 7)).astype(F32).astype(BF)
    for copy in copies:
        copy.wait()
    for k in range(KIDS // tall):
        rows = slice(k * tall, (k + 1) * tall)
        on_tiles = jnp.dot(hot_ref[rows, :LANES], mask, preferred_element_type=F32).astype(BF)
        row_mask = jnp.dot(
            on_tiles * hot_ref[rows, LANES:], expand, preferred_element_type=F32
        ).astype(BF)
        for copy in reads[k * 4 : (k + 1) * 4]:
            copy.wait()
        product_ref[rows, :] = jnp.dot(
            buf_ref[rows, :] * row_mask, held_ref[...], preferred_element_type=F32
        ).astype(BF)
    high = pos >> 8
    writes = []
    for k in range(KIDS // tall):
        for q in range(tall // 256):
            on = (high == k * (tall // 256) + q).astype(F32).astype(BF)
            for b in range(KIDS // LANES):
                at = slice(b * LANES, (b + 1) * LANES)
                perm_ref[k % 2, q * 256 : (q + 1) * 256, at] = low_ref[:, at] * on[b : b + 1, :]
        out = jnp.dot(perm_ref[k % 2], product_ref[...], preferred_element_type=F32).astype(BF)
        for w in range(tall // PAIR):
            for half in range(2):
                stage_ref[k * (tall // PAIR) + w, half] = out[
                    w * PAIR : (w + 1) * PAIR, half * LANES : (half + 1) * LANES
                ]
        at = pl.ds(k * (tall // PAIR), tall // PAIR)
        copy = pltpu.make_async_copy(stage_ref.at[at], out_ref.at[at], out_sems.at[k])
        copy.start()
        writes.append(copy)
    for copy in writes:
        copy.wait()


def child_call(child_map, pos, given, rows, other, probes, probes2):
    return pl.pallas_call(
        child_kernel,
        in_specs=[VM, VM, VM, ANY, ANY, ANY, ANY],
        out_specs=ANY,
        out_shape=jax.ShapeDtypeStruct((WIDE, 2, PAIR, LANES), BF),
        scratch_shapes=[
            pltpu.VMEM((1024, 256), BF),
            pltpu.VMEM((KIDS, 1024), BF),
            pltpu.VMEM((KIDS, 256), BF),
            pltpu.VMEM((256, KIDS), BF),
            pltpu.VMEM((KIDS, 256), BF),
            pltpu.VMEM((2, 1024, KIDS), BF),
            pltpu.VMEM((WIDE, 2, PAIR, LANES), BF),
            pltpu.SemaphoreType.DMA((4,)),
            pltpu.SemaphoreType.DMA((4, 2)),
            pltpu.SemaphoreType.DMA((2,)),
        ],
        compiler_params=params(58),
        cost_estimate=LONG,
        name="child_product",
    )(child_map, pos, given, rows, other, probes, probes2)


def gather_lanes(ints_ref):
    lane = iota((KIDS // LANES, LANES), 1) >> 5
    out = jnp.zeros((KIDS // LANES, LANES), I32)
    for q in range(4):
        out = jnp.where(lane == q, ints_ref[pl.ds(q, KIDS // LANES, stride=4), 0, 0, :], out)
    return out


def cross_kernel(keep_ref, core_ref, out_ref):
    out_ref[...] = (keep_ref[...].astype(F32) + core_ref[:, :LANES].astype(F32)).astype(BF)


def cross_call(keep, core):
    return pl.pallas_call(
        cross_kernel,
        in_specs=[VM, VM],
        out_specs=VM,
        out_shape=jax.ShapeDtypeStruct((ROWS, LANES), BF),
        compiler_params=params(8),
        cost_estimate=SHORT,
        name="core_sum",
    )(keep, core)


def own_kernel(ints_ref, keep_ref, core_ref, far_ref, out_ref, low_ref, high_ref):
    out_ref[...] = (
        keep_ref[...].astype(F32) + core_ref[:, LANES:].astype(F32) + far_ref[...].astype(F32)
    )
    place = gather_lanes(ints_ref)
    high_ref[...] = place >> 8
    low = place & 255
    row = iota((256, LANES), 0)
    for b in range(KIDS // LANES):
        low_ref[:, b * LANES : (b + 1) * LANES] = (
            (low[b : b + 1, :] == row).astype(F32).astype(BF)
        )


def own_call(ints, keep, core, far):
    return pl.pallas_call(
        own_kernel,
        in_specs=[VM] * 4,
        out_specs=[VM] * 3,
        out_shape=[
            jax.ShapeDtypeStruct((ROWS, LANES), F32),
            jax.ShapeDtypeStruct((256, KIDS), BF),
            jax.ShapeDtypeStruct((KIDS // LANES, LANES), I32),
        ],
        compiler_params=params(8),
        cost_estimate=LONG,
        name="own_sum",
    )(ints, keep, core, far)


def final_kernel(
    low_ref, high_ref, own_ref, came_ref, out_ref, held_ref, hot_ref, stage_ref, out_sems
):
    for w in range(WIDE):
        for half in range(2):
            held_ref[w * PAIR : (w + 1) * PAIR, half * LANES : (half + 1) * LANES] = came_ref[
                w, half
            ]
    high = high_ref[...]
    tall = 1024
    writes = []
    for k in range(ROWS // tall):
        for q in range(tall // 256):
            on = (high == k * (tall // 256) + q).astype(F32).astype(BF)
            for b in range(KIDS // LANES):
                at = slice(b * LANES, (b + 1) * LANES)
                hot_ref[k % 2, q * 256 : (q + 1) * 256, at] = low_ref[:, at] * on[b : b + 1, :]
        added = jnp.dot(hot_ref[k % 2], held_ref[...], preferred_element_type=F32)
        rows = slice(k * tall, (k + 1) * tall)
        stage_ref[rows, :] = (own_ref[rows, :] + (added[:, :LANES] + added[:, LANES:])).astype(BF)
        at = pl.ds(k * tall, tall)
        copy = pltpu.make_async_copy(stage_ref.at[at], out_ref.at[at], out_sems.at[k])
        copy.start()
        writes.append(copy)
    for copy in writes:
        copy.wait()


def final_call(low, high, own, came):
    return pl.pallas_call(
        final_kernel,
        in_specs=[VM] * 4,
        out_specs=ANY,
        out_shape=jax.ShapeDtypeStruct((ROWS, LANES), BF),
        scratch_shapes=[
            pltpu.VMEM((KIDS, 256), BF),
            pltpu.VMEM((2, 1024, KIDS), BF),
            pltpu.VMEM((ROWS, LANES), BF),
            pltpu.SemaphoreType.DMA((3,)),
        ],
        compiler_params=params(20),
        cost_estimate=SHORT,
        name="scatter_sum",
    )(low, high, own, came)


SWAP = [(0, 1), (1, 0)]


def local(parent_front, child_updates, child_map, tile_mask, probes):
    child_map = child_map.reshape(KIDS // LANES, LANES)
    other = lax.ppermute(child_updates, "c", SWAP)
    probes2 = lax.ppermute(probes, "c", SWAP)
    pos, mine = rank_call(child_map, tile_mask)
    given = lax.all_to_all(
        mine.reshape(2 * WIDE, 2, LANES), WIDE_AXES + ("c",), split_axis=0, concat_axis=0, tiled=True
    ).reshape(WIDE, 2, 2, LANES)
    far_keep, own_keep, send = parent_call(tile_mask, parent_front, probes)
    given, other, probes2, send = lax.optimization_barrier((given, other, probes2, send))
    core = lax.ppermute(send, "c", SWAP)
    kid = child_call(child_map, pos, given, child_updates, other, probes, probes2)
    kid, core = lax.optimization_barrier((kid, core))
    crossing = cross_call(far_keep, core)
    far = lax.ppermute(crossing, "h", SWAP)
    came = lax.all_to_all(
        kid.reshape(2 * WIDE, PAIR, LANES), WIDE_AXES + ("h",), split_axis=0, concat_axis=0, tiled=True
    ).reshape(WIDE, 2, PAIR, LANES)
    own, low2, high2 = own_call(given, own_keep, core, far)
    return final_call(low2, high2, own, came)


def solution(mesh):
    fine = Mesh(mesh.devices.reshape(8, 2, 4, 2, 2), ("z", "l", "y", "h", "c"))
    both = P(WIDE_AXES, ("h", "c"))
    placed = (both, both, P(WIDE_AXES), both, P(("h", "c"), None))
    return jax.shard_map(local, mesh=fine, in_specs=placed, out_specs=both, check_vma=False)
```

```python
import jax
import jax.numpy as jnp
from jax import lax
from jax.experimental import pallas as pl
from jax.experimental.pallas import tpu as pltpu
from jax.sharding import Mesh, PartitionSpec as P

BF = jnp.bfloat16
F32 = jnp.float32
I32 = jnp.int32
ROWS = 3072
KIDS = 2048
WIDE = 64
PAIR = 32
LANES = 128
MIB = 1 << 20
WIDE_AXES = ("z", "l", "y")


def iota(shape, dim):
    return lax.broadcasted_iota(I32, shape, dim)


def params(mib):
    return pltpu.CompilerParams(vmem_limit_bytes=mib * MIB)


def split_map(child_map):
    target = (lax.shift_right_logical(child_map, 10) * 171) >> 9
    return target, child_map - target * ROWS


def rank_kernel(map_ref, mask_ref, mask2_ref, pos_ref, out_ref, hot_ref, val_ref):
    target, place = split_map(map_ref[...])
    blocks = KIDS // LANES
    upper = (iota((LANES, 2 * LANES), 0) < iota((LANES, 2 * LANES), 1)).astype(F32).astype(BF)
    carry = jnp.zeros((WIDE, LANES), F32)
    lane_rank = (iota((LANES, LANES), 0) & (PAIR - 1)).astype(F32)
    for b in range(blocks):
        at = pl.ds(b * LANES, LANES)
        hot = (iota((WIDE, LANES), 0) == target[b : b + 1, :]).astype(F32)
        hot_ref[:, at] = hot.astype(BF)
        sums = jnp.dot(hot.astype(BF), upper, preferred_element_type=F32)
        rank = jnp.sum(hot * (sums[:, :LANES] + carry), axis=0, keepdims=True)
        carry = carry + sums[:, LANES:]
        pos_ref[b : b + 1, :] = target[b : b + 1, :] * PAIR + rank.astype(I32)
        chosen = lane_rank == rank
        high = (place[b : b + 1, :] >> 6).astype(F32)
        low = (place[b : b + 1, :] & 63).astype(F32)
        val_ref[:LANES, at] = jnp.where(chosen, high, 0.0).astype(BF)
        val_ref[LANES:, at] = jnp.where(chosen, low, 0.0).astype(BF)
    both = lax.dot_general(
        hot_ref[...], val_ref[...], (((1,), (1,)), ((), ())), preferred_element_type=F32
    )
    places = (both[:, :LANES] * 64.0 + both[:, LANES:]).astype(I32)
    lane = iota((12, LANES), 1)
    row = iota((12, LANES), 0)
    flat = jnp.zeros((1, LANES), I32)
    for first, ref in ((0, mask_ref), (64, mask2_ref)):
        for t in range(4):
            flat += jnp.sum(
                jnp.where(lane == first + row * 4 + t, ref[:, t : t + 1], 0), axis=0, keepdims=True
            )
    out_ref[:, 0, :] = places
    out_ref[:, 1, :] = jnp.broadcast_to(flat, (WIDE, LANES))


def rank_call(child_map, tile_mask, tile_mask2):
    return pl.pallas_call(
        rank_kernel,
        out_shape=(
            jax.ShapeDtypeStruct((KIDS // LANES, LANES), I32),
            jax.ShapeDtypeStruct((WIDE, 2, LANES), I32),
        ),
        scratch_shapes=[pltpu.VMEM((WIDE, KIDS), BF), pltpu.VMEM((2 * LANES, KIDS), BF)],
        compiler_params=params(58),
        cost_estimate=pl.CostEstimate(flops=1000, bytes_accessed=1000, transcendentals=0),
        name="rank",
    )(child_map, tile_mask, tile_mask2)


def load_probes(src, dst, sem, starts, first=0, first_sem=0):
    rows = pl.ds(first, src.shape[0])
    return [
        pltpu.make_async_copy(
            src.at[:, pl.ds(pl.multiple_of(start * LANES, LANES), LANES)],
            dst.at[rows, pl.ds(k * LANES, LANES)],
            sem.at[first_sem + k],
        )
        for k, start in enumerate(starts)
    ]


PARENT_TALL = 768


def parent_kernel(
    mask_hbm, x_ref, probe_ref, far_keep_ref, own_keep_ref, send_ref,
    held_ref, buf_ref, out_ref, mask_ref, mask_sem, probe_sem, sems, out_sems,
):
    h, c = lax.axis_index("h"), lax.axis_index("c")
    tall = PARENT_TALL
    chunks = ROWS // tall
    probe_copies = load_probes(
        probe_ref,
        held_ref,
        probe_sem,
        [2 * (1 - h) + c, 2 * h + c, 2 * (1 - h) + 1 - c, 2 * h + 1 - c],
    )
    reads = [
        pltpu.make_async_copy(
            x_ref.at[pl.ds(k * 256, 256)], buf_ref.at[pl.ds(k * 256, 256)], sems.at[k]
        )
        for k in range(ROWS // 256)
    ]
    step = tall // 256
    mask_copy = pltpu.make_async_copy(mask_hbm, mask_ref, mask_sem)
    for copy in [mask_copy] + probe_copies + reads[: 2 * step]:
        copy.start()
    for copy in [mask_copy] + probe_copies:
        copy.wait()
    writes = []
    for k in range(chunks):
        for copy in reads[k * step : (k + 1) * step]:
            copy.wait()
        for copy in reads[(k + 2) * step : (k + 3) * step]:
            copy.start()
        masked = jnp.concatenate(
            [
                jnp.concatenate(
                    [
                        jnp.where(
                            mask_ref[r, t] != 0,
                            buf_ref[r * 256 : (r + 1) * 256, t * LANES : (t + 1) * LANES],
                            jnp.zeros((), BF),
                        )
                        for t in range(10)
                    ],
                    axis=1,
                )
                for r in range(k * step, (k + 1) * step)
            ],
            axis=0,
        )
        out_ref[k * tall : (k + 1) * tall, :] = jnp.dot(
            masked, held_ref[...], preferred_element_type=F32
        ).astype(BF)
        at = pl.ds(k * tall, tall)
        for n, (dst, first, wide) in enumerate(
            ((far_keep_ref, 0, LANES), (own_keep_ref, LANES, LANES), (send_ref, 256, 256))
        ):
            copy = pltpu.make_async_copy(
                out_ref.at[at, pl.ds(first, wide)], dst.at[at], out_sems.at[k, n]
            )
            copy.start()
            writes.append(copy)
    for copy in writes:
        copy.wait()


VM = pl.BlockSpec(memory_space=pltpu.VMEM)
ANY = pl.BlockSpec(memory_space=pl.ANY)
LONG = pl.CostEstimate(flops=200 * 10**9, bytes_accessed=64 * MIB, transcendentals=0)
SHORT = pl.CostEstimate(flops=1000, bytes_accessed=1000, transcendentals=0)


def parent_call(tile_mask, front, probes):
    return pl.pallas_call(
        parent_kernel,
        in_specs=[ANY] * 3,
        out_specs=[ANY] * 3,
        out_shape=[
            jax.ShapeDtypeStruct((ROWS, LANES), BF),
            jax.ShapeDtypeStruct((ROWS, LANES), BF),
            jax.ShapeDtypeStruct((ROWS, 256), BF),
        ],
        scratch_shapes=[
            pltpu.VMEM((1280, 512), BF),
            pltpu.VMEM((ROWS, 1280), BF),
            pltpu.VMEM((ROWS, 512), BF),
            pltpu.SMEM((12, 10), I32),
            pltpu.SemaphoreType.DMA,
            pltpu.SemaphoreType.DMA((4,)),
            pltpu.SemaphoreType.DMA((ROWS // 256,)),
            pltpu.SemaphoreType.DMA((ROWS // PARENT_TALL, 3)),
        ],
        compiler_params=params(58),
        cost_estimate=LONG,
        name="parent_product",
    )(tile_mask, front, probes)


def child_kernel(
    map_hbm, pos_hbm, given_hbm, x_ref, other_ref, probe_ref, probe2_ref,
    out_ref, held_ref, buf_ref, hot_ref, low_ref, product_ref, perm_ref, stage_ref,
    map_ref, pos_ref, given_ref, small_sem, probe_sem, sems, out_sems,
):
    c = lax.axis_index("c")
    tall = 1024
    copies = load_probes(probe_ref.at[pl.ds(0, 512)], held_ref, probe_sem, [c, 2 + c])
    copies += load_probes(
        probe2_ref.at[pl.ds(0, 512)], held_ref, probe_sem, [c, 2 + c], 512, 2
    )
    reads = []
    for k in range(4):
        at = pl.ds(k * 512, 512)
        for n, src in enumerate((x_ref, other_ref)):
            reads.append(
                pltpu.make_async_copy(
                    src.at[at], buf_ref.at[at, pl.ds(n * 512, 512)], sems.at[k, n]
                )
            )
    small = [
        pltpu.make_async_copy(src, dst, small_sem.at[k])
        for k, (src, dst) in enumerate(
            ((map_hbm, map_ref), (given_hbm, given_ref), (pos_hbm, pos_ref))
        )
    ]
    for copy in small + reads[:4] + copies + reads[4:]:
        copy.start()
    small[0].wait()

    target, place = split_map(map_ref[...])
    tile = place >> 8
    for b in range(KIDS // LANES):
        rows = slice(b * LANES, (b + 1) * LANES)
        hot = (iota((LANES, LANES), 0) == target[b : b + 1, :]).astype(F32)
        hot_ref[rows, :LANES] = hot.T.astype(BF)
        on = (((iota((LANES, LANES), 0) & 63) >> 2) == tile[b : b + 1, :]).astype(F32)
        hot_ref[rows, LANES:] = on.T.astype(BF)

    small[1].wait()
    mask = given_ref[:, 1, :].astype(F32).astype(BF)
    mask = jnp.concatenate([mask, jnp.zeros((WIDE, LANES), BF)], axis=0)
    lane, col = iota((LANES, 1024), 0), iota((LANES, 1024), 1)
    expand = ((lane >> 6) * 4 + (lane & 3) == (col >> 7)).astype(F32).astype(BF)
    for copy in copies:
        copy.wait()
    for k in range(KIDS // tall):
        rows = slice(k * tall, (k + 1) * tall)
        on_tiles = jnp.dot(hot_ref[rows, :LANES], mask, preferred_element_type=F32).astype(BF)
        row_mask = jnp.dot(
            on_tiles * hot_ref[rows, LANES:], expand, preferred_element_type=F32
        ).astype(BF)
        for copy in reads[k * 4 : (k + 1) * 4]:
            copy.wait()
        product_ref[rows, :] = jnp.dot(
            buf_ref[rows, :] * row_mask, held_ref[...], preferred_element_type=F32
        ).astype(BF)
    small[2].wait()
    pos = pos_ref[...]
    low, high = pos & 255, pos >> 8
    for b in range(KIDS // LANES):
        low_ref[:, b * LANES : (b + 1) * LANES] = (
            (iota((256, LANES), 0) == low[b : b + 1, :]).astype(F32).astype(BF)
        )
    writes = []
    for k in range(KIDS // tall):
        for q in range(tall // 256):
            on = (high == k * (tall // 256) + q).astype(F32).astype(BF)
            for b in range(KIDS // LANES):
                at = slice(b * LANES, (b + 1) * LANES)
                perm_ref[k % 2, q * 256 : (q + 1) * 256, at] = low_ref[:, at] * on[b : b + 1, :]
        out = jnp.dot(perm_ref[k % 2], product_ref[...], preferred_element_type=F32).astype(BF)
        for w in range(tall // PAIR):
            for half in range(2):
                stage_ref[k * (tall // PAIR) + w, half] = out[
                    w * PAIR : (w + 1) * PAIR, half * LANES : (half + 1) * LANES
                ]
        at = pl.ds(k * (tall // PAIR), tall // PAIR)
        copy = pltpu.make_async_copy(stage_ref.at[at], out_ref.at[at], out_sems.at[k])
        copy.start()
        writes.append(copy)
    for copy in writes:
        copy.wait()


def child_call(child_map, pos, given, rows, other, probes, probes2):
    return pl.pallas_call(
        child_kernel,
        in_specs=[ANY] * 7,
        out_specs=ANY,
        out_shape=jax.ShapeDtypeStruct((WIDE, 2, PAIR, LANES), BF),
        scratch_shapes=[
            pltpu.VMEM((1024, 256), BF),
            pltpu.VMEM((KIDS, 1024), BF),
            pltpu.VMEM((KIDS, 256), BF),
            pltpu.VMEM((256, KIDS), BF),
            pltpu.VMEM((KIDS, 256), BF),
            pltpu.VMEM((2, 1024, KIDS), BF),
            pltpu.VMEM((WIDE, 2, PAIR, LANES), BF),
            pltpu.VMEM((KIDS // LANES, LANES), I32),
            pltpu.VMEM((KIDS // LANES, LANES), I32),
            pltpu.VMEM((WIDE, 2, LANES), I32),
            pltpu.SemaphoreType.DMA((3,)),
            pltpu.SemaphoreType.DMA((4,)),
            pltpu.SemaphoreType.DMA((4, 2)),
            pltpu.SemaphoreType.DMA((2,)),
        ],
        compiler_params=params(58),
        cost_estimate=LONG,
        name="child_product",
    )(child_map, pos, given, rows, other, probes, probes2)


def gather_lanes(ints_ref):
    lane = iota((KIDS // LANES, LANES), 1) >> 5
    out = jnp.zeros((KIDS // LANES, LANES), I32)
    for q in range(4):
        out = jnp.where(lane == q, ints_ref[pl.ds(q, KIDS // LANES, stride=4), 0, :], out)
    return out


def cross_kernel(keep_ref, core_ref, out_ref):
    out_ref[...] = (keep_ref[...].astype(F32) + core_ref[:, :LANES].astype(F32)).astype(BF)


def cross_call(keep, core):
    return pl.pallas_call(
        cross_kernel,
        in_specs=[VM, VM],
        out_specs=VM,
        out_shape=jax.ShapeDtypeStruct((ROWS, LANES), BF),
        compiler_params=params(8),
        cost_estimate=SHORT,
        name="core_sum",
    )(keep, core)


def own_kernel(ints_ref, keep_ref, core_ref, far_ref, out_ref, low_ref, high_ref):
    out_ref[...] = (
        keep_ref[...].astype(F32) + core_ref[:, LANES:].astype(F32) + far_ref[...].astype(F32)
    )
    place = gather_lanes(ints_ref)
    high = (place >> 8).astype(F32)
    low = place & 255
    row = iota((256, LANES), 0)
    for b in range(KIDS // LANES):
        at = slice(b * LANES, (b + 1) * LANES)
        low_ref[:, at] = (low[b : b + 1, :] == row).astype(F32).astype(BF)
        high_ref[at, :] = jnp.broadcast_to(high[b : b + 1, :], (LANES, LANES)).T.astype(BF)


def own_call(ints, keep, core, far):
    return pl.pallas_call(
        own_kernel,
        in_specs=[VM] * 4,
        out_specs=[VM] * 3,
        out_shape=[
            jax.ShapeDtypeStruct((ROWS, LANES), F32),
            jax.ShapeDtypeStruct((256, KIDS), BF),
            jax.ShapeDtypeStruct((KIDS, LANES), BF),
        ],
        compiler_params=params(8),
        cost_estimate=LONG,
        name="own_sum",
    )(ints, keep, core, far)


def final_kernel(
    low_ref, high_ref, own_ref, came_ref, out_ref, sum_ref, part_ref, stage_ref, out_sems
):
    for w in range(WIDE):
        sum_ref[w * PAIR : (w + 1) * PAIR, :] = (
            came_ref[w, 0].astype(F32) + came_ref[w, 1].astype(F32)
        ).astype(BF)
    writes = []
    for k in range(ROWS // 512):
        for q in range(2):
            part_ref[k % 2, :, q * LANES : (q + 1) * LANES] = jnp.where(
                high_ref[...] == 2 * k + q, sum_ref[...], jnp.zeros((), BF)
            )
        added = jnp.dot(low_ref[...], part_ref[k % 2], preferred_element_type=F32)
        for q in range(2):
            rows = slice((2 * k + q) * 256, (2 * k + q + 1) * 256)
            stage_ref[rows, :] = (
                own_ref[rows, :] + added[:, q * LANES : (q + 1) * LANES]
            ).astype(BF)
        at = pl.ds(k * 512, 512)
        copy = pltpu.make_async_copy(stage_ref.at[at], out_ref.at[at], out_sems.at[k])
        copy.start()
        writes.append(copy)
    for copy in writes:
        copy.wait()


def final_call(low, high, own, came):
    return pl.pallas_call(
        final_kernel,
        in_specs=[VM] * 4,
        out_specs=ANY,
        out_shape=jax.ShapeDtypeStruct((ROWS, LANES), BF),
        scratch_shapes=[
            pltpu.VMEM((KIDS, LANES), BF),
            pltpu.VMEM((2, KIDS, 256), BF),
            pltpu.VMEM((ROWS, LANES), BF),
            pltpu.SemaphoreType.DMA((ROWS // 512,)),
        ],
        compiler_params=params(20),
        cost_estimate=SHORT,
        name="scatter_sum",
    )(low, high, own, came)


SWAP = [(0, 1), (1, 0)]


def local(parent_front, child_updates, child_map, tile_mask, probes):
    child_map = child_map.reshape(KIDS // LANES, LANES)
    other = lax.ppermute(child_updates, "c", SWAP)
    probes2 = lax.ppermute(probes, "c", SWAP)
    pos, mine = rank_call(child_map, tile_mask, lax.ppermute(tile_mask, "c", SWAP))
    given = lax.all_to_all(mine, WIDE_AXES, split_axis=0, concat_axis=0, tiled=True)
    far_keep, own_keep, send = parent_call(tile_mask, parent_front, probes)
    given, other, probes2, send = lax.optimization_barrier((given, other, probes2, send))
    core = lax.ppermute(send, "c", SWAP)
    kid = child_call(child_map, pos, given, child_updates, other, probes, probes2)
    kid, core = lax.optimization_barrier((kid, core))
    crossing = cross_call(far_keep, core)
    far = lax.ppermute(crossing, "h", SWAP)
    came = lax.all_to_all(
        kid.reshape(2 * WIDE, PAIR, LANES), WIDE_AXES + ("h",), split_axis=0, concat_axis=0, tiled=True
    ).reshape(WIDE, 2, PAIR, LANES)
    own, low2, high2 = own_call(given, own_keep, core, far)
    return final_call(low2, high2, own, came)


def solution(mesh):
    fine = Mesh(mesh.devices.reshape(8, 2, 4, 2, 2), ("z", "l", "y", "h", "c"))
    both = P(WIDE_AXES, ("h", "c"))
    placed = (both, both, P(WIDE_AXES), both, P(("h", "c"), None))
    return jax.shard_map(local, mesh=fine, in_specs=placed, out_specs=both, check_vma=False)
```

```python
import jax
import jax.numpy as jnp
from jax import lax
from jax.experimental import pallas as pl
from jax.experimental.pallas import tpu as pltpu
from jax.sharding import Mesh, PartitionSpec as P

BF = jnp.bfloat16
F32 = jnp.float32
I32 = jnp.int32
ROWS = 3072
KIDS = 2048
WIDE = 64
PAIR = 32
LANES = 128
MIB = 1 << 20
WIDE_AXES = ("z", "l", "y")


def iota(shape, dim):
    return lax.broadcasted_iota(I32, shape, dim)


def params(mib):
    return pltpu.CompilerParams(vmem_limit_bytes=mib * MIB)


def split_map(child_map):
    target = (lax.shift_right_logical(child_map, 10) * 171) >> 9
    return target, child_map - target * ROWS


def rank_kernel(map_ref, mask_ref, mask2_ref, pos_ref, out_ref, hot_ref, val_ref):
    target, place = split_map(map_ref[...])
    blocks = KIDS // LANES
    upper = (iota((LANES, 2 * LANES), 0) < iota((LANES, 2 * LANES), 1)).astype(F32).astype(BF)
    carry = jnp.zeros((WIDE, LANES), F32)
    lane_rank = (iota((LANES, LANES), 0) & (PAIR - 1)).astype(F32)
    for b in range(blocks):
        at = pl.ds(b * LANES, LANES)
        hot = (iota((WIDE, LANES), 0) == target[b : b + 1, :]).astype(F32)
        hot_ref[:, at] = hot.astype(BF)
        sums = jnp.dot(hot.astype(BF), upper, preferred_element_type=F32)
        rank = jnp.sum(hot * (sums[:, :LANES] + carry), axis=0, keepdims=True)
        carry = carry + sums[:, LANES:]
        pos_ref[b : b + 1, :] = target[b : b + 1, :] * PAIR + rank.astype(I32)
        chosen = lane_rank == rank
        high = (place[b : b + 1, :] >> 6).astype(F32)
        low = (place[b : b + 1, :] & 63).astype(F32)
        val_ref[:LANES, at] = jnp.where(chosen, high, 0.0).astype(BF)
        val_ref[LANES:, at] = jnp.where(chosen, low, 0.0).astype(BF)
    both = lax.dot_general(
        hot_ref[...], val_ref[...], (((1,), (1,)), ((), ())), preferred_element_type=F32
    )
    places = (both[:, :LANES] * 64.0 + both[:, LANES:]).astype(I32)
    lane = iota((12, LANES), 1)
    row = iota((12, LANES), 0)
    flat = jnp.zeros((1, LANES), I32)
    for first, ref in ((0, mask_ref), (64, mask2_ref)):
        for t in range(4):
            flat += jnp.sum(
                jnp.where(lane == first + row * 4 + t, ref[:, t : t + 1], 0), axis=0, keepdims=True
            )
    out_ref[:, 0, :] = places
    out_ref[:, 1, :] = jnp.broadcast_to(flat, (WIDE, LANES))


def rank_call(child_map, tile_mask, tile_mask2):
    return pl.pallas_call(
        rank_kernel,
        out_shape=(
            jax.ShapeDtypeStruct((KIDS // LANES, LANES), I32),
            jax.ShapeDtypeStruct((WIDE, 2, LANES), I32),
        ),
        scratch_shapes=[pltpu.VMEM((WIDE, KIDS), BF), pltpu.VMEM((2 * LANES, KIDS), BF)],
        compiler_params=params(58),
        cost_estimate=pl.CostEstimate(flops=1000, bytes_accessed=1000, transcendentals=0),
        name="rank",
    )(child_map, tile_mask, tile_mask2)


def load_probes(src, dst, sem, starts, first=0, first_sem=0):
    rows = pl.ds(first, src.shape[0])
    return [
        pltpu.make_async_copy(
            src.at[:, pl.ds(pl.multiple_of(start * LANES, LANES), LANES)],
            dst.at[rows, pl.ds(k * LANES, LANES)],
            sem.at[first_sem + k],
        )
        for k, start in enumerate(starts)
    ]


PARENT_TALL = 768


def parent_kernel(
    mask_hbm, x_ref, probe_ref, far_keep_ref, own_keep_ref, send_ref,
    held_ref, buf_ref, out_ref, mask_ref, mask_sem, probe_sem, sems, out_sems,
):
    h, c = lax.axis_index("h"), lax.axis_index("c")
    tall = PARENT_TALL
    chunks = ROWS // tall
    probe_copies = load_probes(
        probe_ref,
        held_ref,
        probe_sem,
        [2 * (1 - h) + c, 2 * h + c, 2 * (1 - h) + 1 - c, 2 * h + 1 - c],
    )
    reads = [
        pltpu.make_async_copy(
            x_ref.at[pl.ds(k * 256, 256)], buf_ref.at[pl.ds(k * 256, 256)], sems.at[k]
        )
        for k in range(ROWS // 256)
    ]
    step = tall // 256
    mask_copy = pltpu.make_async_copy(mask_hbm, mask_ref, mask_sem)
    for copy in [mask_copy] + probe_copies + reads[: 2 * step]:
        copy.start()
    for copy in [mask_copy] + probe_copies:
        copy.wait()
    writes = []
    for k in range(chunks):
        for copy in reads[k * step : (k + 1) * step]:
            copy.wait()
        for copy in reads[(k + 2) * step : (k + 3) * step]:
            copy.start()
        masked = jnp.concatenate(
            [
                jnp.concatenate(
                    [
                        jnp.where(
                            mask_ref[r, t] != 0,
                            buf_ref[r * 256 : (r + 1) * 256, t * LANES : (t + 1) * LANES],
                            jnp.zeros((), BF),
                        )
                        for t in range(10)
                    ],
                    axis=1,
                )
                for r in range(k * step, (k + 1) * step)
            ],
            axis=0,
        )
        out_ref[k * tall : (k + 1) * tall, :] = jnp.dot(
            masked, held_ref[...], preferred_element_type=F32
        ).astype(BF)
        at = pl.ds(k * tall, tall)
        for n, (dst, first, wide) in enumerate(
            ((far_keep_ref, 0, LANES), (own_keep_ref, LANES, LANES), (send_ref, 256, 256))
        ):
            copy = pltpu.make_async_copy(
                out_ref.at[at, pl.ds(first, wide)], dst.at[at], out_sems.at[k, n]
            )
            copy.start()
            writes.append(copy)
    for copy in writes:
        copy.wait()


VM = pl.BlockSpec(memory_space=pltpu.VMEM)
ANY = pl.BlockSpec(memory_space=pl.ANY)
LONG = pl.CostEstimate(flops=200 * 10**9, bytes_accessed=64 * MIB, transcendentals=0)
SHORT = pl.CostEstimate(flops=1000, bytes_accessed=1000, transcendentals=0)


def parent_call(tile_mask, front, probes):
    return pl.pallas_call(
        parent_kernel,
        in_specs=[ANY] * 3,
        out_specs=[ANY] * 3,
        out_shape=[
            jax.ShapeDtypeStruct((ROWS, LANES), BF),
            jax.ShapeDtypeStruct((ROWS, LANES), BF),
            jax.ShapeDtypeStruct((ROWS, 256), BF),
        ],
        scratch_shapes=[
            pltpu.VMEM((1280, 512), BF),
            pltpu.VMEM((ROWS, 1280), BF),
            pltpu.VMEM((ROWS, 512), BF),
            pltpu.SMEM((12, 10), I32),
            pltpu.SemaphoreType.DMA,
            pltpu.SemaphoreType.DMA((4,)),
            pltpu.SemaphoreType.DMA((ROWS // 256,)),
            pltpu.SemaphoreType.DMA((ROWS // PARENT_TALL, 3)),
        ],
        compiler_params=params(58),
        cost_estimate=LONG,
        name="parent_product",
    )(tile_mask, front, probes)


def child_kernel(
    map_hbm, pos_hbm, given_hbm, x_ref, other_ref, probe_ref, probe2_ref,
    out_ref, held_ref, buf_ref, hot_ref, low_ref, product_ref, perm_ref, stage_ref,
    map_ref, pos_ref, given_ref, small_sem, probe_sem, sems, out_sems,
):
    c = lax.axis_index("c")
    tall = 1024
    copies = load_probes(probe_ref.at[pl.ds(0, 512)], held_ref, probe_sem, [c, 2 + c])
    copies += load_probes(
        probe2_ref.at[pl.ds(0, 512)], held_ref, probe_sem, [c, 2 + c], 512, 2
    )
    reads = []
    for k in range(4):
        at = pl.ds(k * 512, 512)
        for n, src in enumerate((x_ref, other_ref)):
            reads.append(
                pltpu.make_async_copy(
                    src.at[at], buf_ref.at[at, pl.ds(n * 512, 512)], sems.at[k, n]
                )
            )
    small = [
        pltpu.make_async_copy(src, dst, small_sem.at[k])
        for k, (src, dst) in enumerate(
            ((map_hbm, map_ref), (given_hbm, given_ref), (pos_hbm, pos_ref))
        )
    ]
    for copy in small + reads[:4] + copies + reads[4:]:
        copy.start()
    small[0].wait()

    target, place = split_map(map_ref[...])
    tile = place >> 8
    for b in range(KIDS // LANES):
        rows = slice(b * LANES, (b + 1) * LANES)
        hot = (iota((LANES, LANES), 0) == target[b : b + 1, :]).astype(F32)
        hot_ref[rows, :LANES] = hot.T.astype(BF)
        on = (((iota((LANES, LANES), 0) & 63) >> 2) == tile[b : b + 1, :]).astype(F32)
        hot_ref[rows, LANES:] = on.T.astype(BF)

    small[1].wait()
    mask = given_ref[:, 1, :].astype(F32).astype(BF)
    mask = jnp.concatenate([mask, jnp.zeros((WIDE, LANES), BF)], axis=0)
    lane, col = iota((LANES, 1024), 0), iota((LANES, 1024), 1)
    expand = ((lane >> 6) * 4 + (lane & 3) == (col >> 7)).astype(F32).astype(BF)
    for copy in copies:
        copy.wait()
    for k in range(KIDS // tall):
        rows = slice(k * tall, (k + 1) * tall)
        on_tiles = jnp.dot(hot_ref[rows, :LANES], mask, preferred_element_type=F32).astype(BF)
        row_mask = jnp.dot(
            on_tiles * hot_ref[rows, LANES:], expand, preferred_element_type=F32
        ).astype(BF)
        for copy in reads[k * 4 : (k + 1) * 4]:
            copy.wait()
        product_ref[rows, :] = jnp.dot(
            buf_ref[rows, :] * row_mask, held_ref[...], preferred_element_type=F32
        ).astype(BF)
    small[2].wait()
    pos = pos_ref[...]
    low, high = pos & 255, pos >> 8
    for b in range(KIDS // LANES):
        low_ref[:, b * LANES : (b + 1) * LANES] = (
            (iota((256, LANES), 0) == low[b : b + 1, :]).astype(F32).astype(BF)
        )
    writes = []
    for k in range(KIDS // tall):
        for q in range(tall // 256):
            on = (high == k * (tall // 256) + q).astype(F32).astype(BF)
            for b in range(KIDS // LANES):
                at = slice(b * LANES, (b + 1) * LANES)
                perm_ref[k % 2, q * 256 : (q + 1) * 256, at] = low_ref[:, at] * on[b : b + 1, :]
        out = jnp.dot(perm_ref[k % 2], product_ref[...], preferred_element_type=F32).astype(BF)
        for w in range(tall // PAIR):
            for half in range(2):
                stage_ref[k * (tall // PAIR) + w, half] = out[
                    w * PAIR : (w + 1) * PAIR, half * LANES : (half + 1) * LANES
                ]
        at = pl.ds(k * (tall // PAIR), tall // PAIR)
        copy = pltpu.make_async_copy(stage_ref.at[at], out_ref.at[at], out_sems.at[k])
        copy.start()
        writes.append(copy)
    for copy in writes:
        copy.wait()


def child_call(child_map, pos, given, rows, other, probes, probes2):
    return pl.pallas_call(
        child_kernel,
        in_specs=[ANY] * 7,
        out_specs=ANY,
        out_shape=jax.ShapeDtypeStruct((WIDE, 2, PAIR, LANES), BF),
        scratch_shapes=[
            pltpu.VMEM((1024, 256), BF),
            pltpu.VMEM((KIDS, 1024), BF),
            pltpu.VMEM((KIDS, 256), BF),
            pltpu.VMEM((256, KIDS), BF),
            pltpu.VMEM((KIDS, 256), BF),
            pltpu.VMEM((2, 1024, KIDS), BF),
            pltpu.VMEM((WIDE, 2, PAIR, LANES), BF),
            pltpu.VMEM((KIDS // LANES, LANES), I32),
            pltpu.VMEM((KIDS // LANES, LANES), I32),
            pltpu.VMEM((WIDE, 2, LANES), I32),
            pltpu.SemaphoreType.DMA((3,)),
            pltpu.SemaphoreType.DMA((4,)),
            pltpu.SemaphoreType.DMA((4, 2)),
            pltpu.SemaphoreType.DMA((2,)),
        ],
        compiler_params=params(58),
        cost_estimate=LONG,
        name="child_product",
    )(child_map, pos, given, rows, other, probes, probes2)


def gather_lanes(ints_ref):
    lane = iota((KIDS // LANES, LANES), 1) >> 5
    out = jnp.zeros((KIDS // LANES, LANES), I32)
    for q in range(4):
        out = jnp.where(lane == q, ints_ref[pl.ds(q, KIDS // LANES, stride=4), 0, :], out)
    return out


def cross_kernel(keep_ref, core_ref, out_ref):
    out_ref[...] = (keep_ref[...].astype(F32) + core_ref[...].astype(F32)).astype(BF)


def cross_call(keep, core):
    part = pl.BlockSpec((ROWS, LANES), lambda i: (0, 0))
    return pl.pallas_call(
        cross_kernel,
        grid=(1,),
        in_specs=[part, part],
        out_specs=part,
        out_shape=jax.ShapeDtypeStruct((ROWS, LANES), BF),
        compiler_params=params(8),
        cost_estimate=SHORT,
        name="core_sum",
    )(keep, core)


def own_kernel(ints_ref, keep_ref, core_ref, far_ref, out_ref, low_ref, high_ref):
    out_ref[...] = (
        keep_ref[...].astype(F32) + core_ref[:, LANES:].astype(F32) + far_ref[...].astype(F32)
    ).astype(BF)
    place = gather_lanes(ints_ref)
    high = (place >> 8).astype(F32)
    low = place & 255
    row = iota((256, LANES), 0)
    for b in range(KIDS // LANES):
        at = slice(b * LANES, (b + 1) * LANES)
        low_ref[:, at] = (low[b : b + 1, :] == row).astype(F32).astype(BF)
        high_ref[at, :] = jnp.broadcast_to(high[b : b + 1, :], (LANES, LANES)).T.astype(BF)


def own_call(ints, keep, core, far):
    return pl.pallas_call(
        own_kernel,
        in_specs=[VM] * 4,
        out_specs=[VM] * 3,
        out_shape=[
            jax.ShapeDtypeStruct((ROWS, LANES), BF),
            jax.ShapeDtypeStruct((256, KIDS), BF),
            jax.ShapeDtypeStruct((KIDS, LANES), BF),
        ],
        compiler_params=params(8),
        cost_estimate=LONG,
        name="own_sum",
    )(ints, keep, core, far)


def final_kernel(
    low_ref, high_ref, own_ref, came_ref, out_ref, sum_ref, part_ref, stage_ref, out_sems
):
    for w in range(WIDE):
        sum_ref[w * PAIR : (w + 1) * PAIR, :] = (
            came_ref[w, 0].astype(F32) + came_ref[w, 1].astype(F32)
        ).astype(BF)
    writes = []
    for k in range(ROWS // 512):
        for q in range(2):
            part_ref[k % 2, :, q * LANES : (q + 1) * LANES] = jnp.where(
                high_ref[...] == 2 * k + q, sum_ref[...], jnp.zeros((), BF)
            )
        added = jnp.dot(low_ref[...], part_ref[k % 2], preferred_element_type=F32)
        for q in range(2):
            rows = slice((2 * k + q) * 256, (2 * k + q + 1) * 256)
            stage_ref[rows, :] = (
                own_ref[rows, :].astype(F32) + added[:, q * LANES : (q + 1) * LANES]
            ).astype(BF)
        at = pl.ds(k * 512, 512)
        copy = pltpu.make_async_copy(stage_ref.at[at], out_ref.at[at], out_sems.at[k])
        copy.start()
        writes.append(copy)
    for copy in writes:
        copy.wait()


def final_call(low, high, own, came):
    return pl.pallas_call(
        final_kernel,
        in_specs=[VM] * 4,
        out_specs=ANY,
        out_shape=jax.ShapeDtypeStruct((ROWS, LANES), BF),
        scratch_shapes=[
            pltpu.VMEM((KIDS, LANES), BF),
            pltpu.VMEM((2, KIDS, 256), BF),
            pltpu.VMEM((ROWS, LANES), BF),
            pltpu.SemaphoreType.DMA((ROWS // 512,)),
        ],
        compiler_params=params(20),
        cost_estimate=SHORT,
        name="scatter_sum",
    )(low, high, own, came)


SWAP = [(0, 1), (1, 0)]


def local(parent_front, child_updates, child_map, tile_mask, probes):
    child_map = child_map.reshape(KIDS // LANES, LANES)
    other = lax.ppermute(child_updates, "c", SWAP)
    probes2 = lax.ppermute(probes, "c", SWAP)
    pos, mine = rank_call(child_map, tile_mask, lax.ppermute(tile_mask, "c", SWAP))
    given = lax.all_to_all(mine, WIDE_AXES, split_axis=0, concat_axis=0, tiled=True)
    far_keep, own_keep, send = parent_call(tile_mask, parent_front, probes)
    given, other, probes2, send = lax.optimization_barrier((given, other, probes2, send))
    core = lax.ppermute(send, "c", SWAP)
    kid = child_call(child_map, pos, given, child_updates, other, probes, probes2)
    kid, core = lax.optimization_barrier((kid, core))
    crossing = cross_call(far_keep, core)
    far = lax.ppermute(crossing, "h", SWAP)
    came = lax.all_to_all(
        kid.reshape(2 * WIDE, PAIR, LANES), WIDE_AXES + ("h",), split_axis=0, concat_axis=0, tiled=True
    ).reshape(WIDE, 2, PAIR, LANES)
    own, low2, high2 = own_call(given, own_keep, core, far)
    return final_call(low2, high2, own, came)


def solution(mesh):
    fine = Mesh(mesh.devices.reshape(8, 2, 4, 2, 2), ("z", "l", "y", "h", "c"))
    both = P(WIDE_AXES, ("h", "c"))
    placed = (both, both, P(WIDE_AXES), both, P(("h", "c"), None))
    return jax.shard_map(local, mesh=fine, in_specs=placed, out_specs=both, check_vma=False)
```
